32 devices in a mesh: dp: 2 (over y), proto: 16 (over z, x, core).
Axes of the slice: x: 2, y: 2, z: 4, core: 2. Of those that a mesh axis runs over, the one named last changes fastest.
Arguments:
- teacher_rows: bfloat16 [128, 256], P(('dp', 'proto')), may hold values from -16 to 16
- student_rows: bfloat16 [128, 256], P(('dp', 'proto')), may hold values from -16 to 16
- teacher_protos: bfloat16 [131072, 256], P(('dp', 'proto')), may hold values from -0.5 to 0.5
- student_protos: bfloat16 [131072, 256], P(('dp', 'proto')), may hold values from -0.5 to 0.5
Outputs:
- row_loss: float32 [128], P(('dp', 'proto'))
- student_grad: float32 [128, 256], P(('dp', 'proto'))
- proto_grad: float32 [131072, 256], P(('dp', 'proto'))
The draws below stay inside these ranges and needn't reach their ends.
All inputs are finite; a program needn't handle non-finite values.
Results may differ from the reference program's by a relative error of at most 0.0008.
The reference program's roundings to bfloat16 on the way count: a program that leaves them out, or rounds other values in their place, can miss the bound.
Values may be sent and summed in bfloat16 or wider, within the bound.
A program may use at most 64 MiB of HBM per device.

```python
import math
import jax
import jax.numpy as jnp
from jax import lax

BOTTLE = 256
PROTOS = 131072
BALANCE_ROUNDS = 2
TOKENS = 128


def cluster_means(key):
    return jax.random.normal(jax.random.fold_in(key, 101), (32, BOTTLE), jnp.float32)


def noise_draw(key, shape):
    return jax.random.normal(key, shape, jnp.float32)


def spread_scale(key, count):
    return jnp.ones((count, 1), jnp.float32)


def teacher_row_values(key):
    means = cluster_means(key)
    labels = jax.random.randint(jax.random.fold_in(key, 102), (TOKENS,), 0, 32)
    strength = jax.random.uniform(jax.random.fold_in(key, 103), (TOKENS, 1), jnp.float32, 0.5, 2.0)
    noise = noise_draw(jax.random.fold_in(key, 104), (TOKENS, BOTTLE))
    mixed = (strength * means[labels] + noise) / jnp.sqrt(strength * strength + 1.0)
    scale_factors = spread_scale(jax.random.fold_in(key, 105), TOKENS)
    return (mixed, scale_factors)


def teacher_prototype_scores(key):
    means = cluster_means(key)
    proto_labels = jax.random.randint(jax.random.fold_in(key, 204), (PROTOS,), 0, 32)
    repeated = means[proto_labels]
    noise = noise_draw(jax.random.fold_in(key, 201), (PROTOS, BOTTLE))
    mixed = (0.6 * repeated + 0.8 * noise) / math.sqrt(BOTTLE)
    scale_factors = spread_scale(jax.random.fold_in(key, 202), PROTOS)
    return (mixed, scale_factors)


def draw_teacher_rows(key, part):
    value_entries, scale_factors = teacher_row_values(key)
    return jnp.clip(value_entries, -16.0, 16.0).astype(jnp.bfloat16)


def draw_student_rows(key, part):
    value_entries, scale_factors = teacher_row_values(key)
    noise = noise_draw(jax.random.fold_in(key, 106), (TOKENS, BOTTLE))
    return jnp.clip(value_entries + 0.3 * scale_factors * noise, -16.0, 16.0).astype(jnp.bfloat16)


def draw_teacher_protos(key, part):
    value_entries, scale_factors = teacher_prototype_scores(key)
    return jnp.clip(value_entries, -0.5, 0.5).astype(jnp.bfloat16)


def draw_student_protos(key, part):
    value_entries, scale_factors = teacher_prototype_scores(key)
    noise = noise_draw(jax.random.fold_in(key, 203), (PROTOS, BOTTLE))
    return jnp.clip(value_entries + 0.1 * scale_factors * noise / math.sqrt(BOTTLE), -0.5, 0.5).astype(jnp.bfloat16)


def setup_inputs(seed: int = 0) -> dict:
    seeds = jax.random.split(jax.random.key(seed), 5)
    teacher_rows = draw_teacher_rows(jax.random.fold_in(seeds[4], 71), 0)
    student_rows = draw_student_rows(jax.random.fold_in(seeds[4], 71), 0)
    teacher_protos = draw_teacher_protos(jax.random.fold_in(seeds[4], 71), 0)
    student_protos = draw_student_protos(jax.random.fold_in(seeds[4], 71), 0)
    return dict(teacher_rows=teacher_rows, student_rows=student_rows, teacher_protos=teacher_protos, student_protos=student_protos)


TEACH_TEMP = 0.04
STUD_TEMP = 0.1
LOSS_SCALE = 4096.0
EPSILON = 1e-06

def unit_rows(value_entries):
    widened = value_entries.astype(jnp.float32)
    return widened * lax.rsqrt(lax.optimization_barrier(jnp.sum(widened * widened, axis=-1, keepdims=True)) + EPSILON)

def unit_back(value_entries, cotangent):
    widened = value_entries.astype(jnp.float32)
    inverse = lax.rsqrt(lax.optimization_barrier(jnp.sum(widened * widened, axis=-1, keepdims=True)) + EPSILON)
    projected = lax.optimization_barrier(jnp.sum(widened * cotangent, axis=-1, keepdims=True))
    return inverse * cotangent - widened * (inverse * inverse * inverse) * projected

def reference(teacher_rows, student_rows, teacher_protos, student_protos):
    t_unit = unit_rows(teacher_rows).astype(jnp.bfloat16)
    s_unit = unit_rows(student_rows).astype(jnp.bfloat16)
    tw_unit = unit_rows(teacher_protos).astype(jnp.bfloat16)
    sw_unit = unit_rows(student_protos).astype(jnp.bfloat16)
    block_cols = math.gcd(PROTOS, max(1, 2 ** 24 // TOKENS))
    blocks = PROTOS // block_cols
    teach_blocks = tw_unit.reshape(blocks, block_cols, BOTTLE)
    stud_blocks = sw_unit.reshape(blocks, block_cols, BOTTLE)

    def teacher_exponent(protos):
        return jnp.exp(jnp.dot(t_unit, protos.T, preferred_element_type=jnp.float32) / TEACH_TEMP)

    def stud_logits(protos):
        return jnp.dot(s_unit, protos.T, preferred_element_type=jnp.float32) / STUD_TEMP

    def exp_block(protos):
        return lax.optimization_barrier(jnp.sum(jnp.exp(stud_logits(protos)), axis=1))
    exp_total = lax.optimization_barrier(jnp.sum(lax.map(exp_block, stud_blocks), axis=0))
    row_scale = jnp.ones((TOKENS,), jnp.float32)
    col_scale = jnp.ones((blocks, block_cols), jnp.float32)
    for balance_round_index in range(BALANCE_ROUNDS):

        def sweep_block(protos, weights=row_scale):
            expos = teacher_exponent(protos)
            columns = 1.0 / lax.optimization_barrier(jnp.sum(expos * weights[:, None], axis=0))
            return (columns, lax.optimization_barrier(jnp.sum(expos * columns[None, :], axis=1)))
        col_scale, row_parts = lax.map(sweep_block, teach_blocks)
        row_scale = 1.0 / lax.optimization_barrier(jnp.sum(row_parts, axis=0))

    def backward(running, inputs):
        teach_protos, stud_protos, columns = inputs
        targets = row_scale[:, None] * teacher_exponent(teach_protos) * columns[None, :]
        logits = stud_logits(stud_protos)
        gradient = (LOSS_SCALE * (jnp.exp(logits) / exp_total[:, None] - targets) / STUD_TEMP).astype(jnp.bfloat16)
        running = running + jnp.dot(gradient, stud_protos, preferred_element_type=jnp.float32)
        proto_part = jnp.dot(gradient.T, s_unit, preferred_element_type=jnp.float32)
        return (running, (proto_part, lax.optimization_barrier(jnp.sum(targets * logits, axis=1))))
    row_cot, (proto_parts, dot_parts) = lax.scan(backward, jnp.zeros((TOKENS, BOTTLE), jnp.float32), (teach_blocks, stud_blocks, col_scale))
    row_loss = jnp.log(exp_total) - lax.optimization_barrier(jnp.sum(dot_parts, axis=0))
    student_grad = unit_back(student_rows, row_cot)
    proto_grad = unit_back(student_protos, proto_parts.reshape(PROTOS, BOTTLE))
    return (row_loss, student_grad, proto_grad)
```

```python
import functools

import jax
import jax.numpy as jnp
from jax import lax
from jax.experimental import pallas as pl
from jax.experimental.pallas import tpu as pltpu
from jax.sharding import PartitionSpec as P

TEACH_TEMP = 0.04
STUD_TEMP = 0.1
LOSS_SCALE = 4096.0
EPSILON = 1e-06
AXES = ("dp", "proto")
LANES = 128
LOAD_PARTS = 4


def inverse_norm(x):
    return lax.rsqrt(jnp.sum(x * x, axis=-1, keepdims=True) + EPSILON)


def fold_lanes(x):
    total = x[:, :LANES]
    for start in range(LANES, x.shape[1], LANES):
        total = total + x[:, start:start + LANES]
    return total


def eye():
    shape = (LANES, LANES)
    return lax.broadcasted_iota(jnp.int32, shape, 0) == lax.broadcasted_iota(jnp.int32, shape, 1)


def to_lanes(column):
    blocks = [
        jnp.sum(jnp.where(eye(), column[i:i + LANES], 0.0), axis=0, keepdims=True)
        for i in range(0, column.shape[0], LANES)
    ]
    return blocks[0] if len(blocks) == 1 else jnp.concatenate(blocks, axis=1)


def to_column(row):
    blocks = [
        jnp.sum(jnp.where(eye(), row[:, i:i + LANES], 0.0), axis=1, keepdims=True)
        for i in range(0, row.shape[1], LANES)
    ]
    return blocks[0] if len(blocks) == 1 else jnp.concatenate(blocks, axis=0)


def kernel(
    dp, proto, cols,
    t_ref, s_ref, tw_hbm, sw_hbm,
    loss_ref, sgrad_ref, pgrad_ref,
    tw_raw, sw_raw, tw_unit, sw_unit, sw_inv, texp, logit, delta,
    rows_buf, sums1, sums2, part, landed, t_all, s_all, col_ref,
    load_sem, send_sem, recv_sem,
):
    n = dp * proto
    own = t_ref.shape[0]
    total_rows = n * own
    width = t_ref.shape[1]
    count = tw_raw.shape[0]
    chunks = count // cols
    me = lax.axis_index("dp") * proto + lax.axis_index("proto")

    def coords(j):
        peer = lax.rem(me + j, n)
        return peer, (lax.div(peer, proto), lax.rem(peer, proto))

    piece = count // LOAD_PARTS
    loads = []
    for k in range(LOAD_PARTS):
        for index, (hbm, raw) in enumerate(((tw_hbm, tw_raw), (sw_hbm, sw_raw))):
            span = pl.ds(k * piece, piece)
            copy = pltpu.make_async_copy(hbm.at[span], raw.at[span], load_sem.at[index, k])
            copy.start()
            loads.append(copy)

    barrier = pltpu.get_barrier_semaphore()

    @pl.loop(1, n)
    def _(j):
        pl.semaphore_signal(barrier, inc=1, device_id=coords(j)[1], device_id_type=pl.DeviceIdType.MESH)

    t_own = t_ref[...].astype(jnp.float32)
    s_own = s_ref[...].astype(jnp.float32)
    s_own_inv = inverse_norm(s_own)
    t_rounded = (t_own * inverse_norm(t_own)).astype(jnp.bfloat16).astype(jnp.float32)
    s_rounded = (s_own * s_own_inv).astype(jnp.bfloat16).astype(jnp.float32)
    rows_buf[me] = jnp.concatenate([t_rounded, s_rounded], axis=0)
    pl.semaphore_wait(barrier, n - 1)

    def spread(phase, source, target):
        @pl.loop(1, n)
        def _(j):
            peer, device = coords(j)
            pltpu.make_async_remote_copy(
                src_ref=source(peer), dst_ref=target.at[me],
                send_sem=send_sem.at[phase], recv_sem=recv_sem.at[phase],
                device_id=device, device_id_type=pl.DeviceIdType.MESH,
            ).start()

    def whole(phase, target):
        span = pl.ds(0, n - 1)
        return pltpu.make_async_remote_copy(
            src_ref=target.at[span], dst_ref=target.at[span],
            send_sem=send_sem.at[phase], recv_sem=recv_sem.at[phase],
            device_id=coords(1)[1], device_id_type=pl.DeviceIdType.MESH,
        )

    spread(0, lambda peer: rows_buf.at[me], rows_buf)

    norm_rows = min(piece, 256)
    for k in range(LOAD_PARTS):
        for index, raw in enumerate((tw_raw, sw_raw)):
            loads[2 * k + index].wait()

            @pl.loop(0, piece // norm_rows)
            def _(c, k=k, index=index, raw=raw):
                span = pl.ds(pl.multiple_of(k * piece + c * norm_rows, norm_rows), norm_rows)
                x = raw[span].astype(jnp.float32)
                inverse = inverse_norm(x)
                unit = (x * inverse).astype(jnp.bfloat16)
                if index == 0:
                    tw_unit[span] = unit
                else:
                    sw_unit[span] = unit
                    sw_inv[span] = jnp.broadcast_to(inverse, (norm_rows, LANES))

    whole(0, rows_buf).wait_recv()
    paired = rows_buf[...].reshape(n // 2, 2, 2 * own, width)
    first, second = paired[:, 0], paired[:, 1]
    upper = lax.broadcasted_iota(jnp.int32, first.shape, 1) < own
    t_all[...] = jnp.where(upper, first, pltpu.roll(second, own, 1)).reshape(total_rows, width).astype(jnp.bfloat16)
    s_all[...] = jnp.where(upper, pltpu.roll(first, own, 1), second).reshape(total_rows, width).astype(jnp.bfloat16)

    transposed = (((1,), (1,)), ((), ()))
    zeros = jnp.zeros((total_rows, LANES), jnp.float32)

    def span_of(c):
        return pl.ds(pl.multiple_of(c * cols, cols), cols)

    def first_pass(c, carry):
        row_sum, exp_sum = carry
        span = span_of(c)
        expo = jnp.exp(
            lax.dot_general(t_all[...], tw_unit[span], transposed, preferred_element_type=jnp.float32)
            * (1.0 / TEACH_TEMP)
        )
        texp[:, span] = expo
        scale = 1.0 / jnp.sum(expo, axis=0, keepdims=True)
        row_sum = row_sum + fold_lanes(expo * scale)
        logits = lax.dot_general(
            s_all[...], sw_unit[span], transposed, preferred_element_type=jnp.float32
        ) * (1.0 / STUD_TEMP)
        logit[:, span] = logits
        exp_sum = exp_sum + fold_lanes(jnp.exp(logits))
        return row_sum, exp_sum

    def share(phase, sums, one, two):
        sums[me] = jnp.concatenate(
            [to_lanes(jnp.sum(x, axis=1, keepdims=True)) for x in (one, two)], axis=0
        )
        spread(phase, lambda peer: sums.at[me], sums)
        whole(phase, sums).wait_recv()
        total = jnp.sum(sums[...], axis=0)
        return total[0:1], total[1:2]

    row_sum, exp_sum = lax.fori_loop(0, chunks, first_pass, (zeros, zeros))
    row_total, exp_total = share(1, sums1, row_sum, exp_sum)
    row_scale = to_column(1.0 / row_total)

    def second_pass(c, carry):
        row_sum, dot_sum = carry
        span = span_of(c)
        expo = texp[:, span]
        scale = 1.0 / jnp.sum(expo * row_scale, axis=0, keepdims=True)
        scaled = expo * scale
        texp[:, span] = scaled
        return row_sum + fold_lanes(scaled), dot_sum + fold_lanes(scaled * logit[:, span])

    row_sum, dot_sum = lax.fori_loop(0, chunks, second_pass, (zeros, zeros))
    row_total, dot_total = share(2, sums2, row_sum, dot_sum)
    factor = LOSS_SCALE / STUD_TEMP
    row_scale = to_column(factor / row_total)
    exp_scale = to_column(factor / exp_total)

    def third_pass(c, carry):
        span = span_of(c)
        gradient = (jnp.exp(logit[:, span]) * exp_scale - texp[:, span] * row_scale).astype(jnp.bfloat16)
        delta[:, span] = gradient
        return carry + jnp.dot(gradient, sw_unit[span], preferred_element_type=jnp.float32)

    row_part = lax.fori_loop(0, chunks, third_pass, jnp.zeros((total_rows, width), jnp.float32))
    part[...] = row_part.reshape(n, own, width)
    landed[me] = part[me]
    spread(3, lambda peer: part.at[peer], landed)

    loss = jnp.log(exp_total) - dot_total / row_total
    shape = (total_rows, LANES)
    mine = lax.broadcasted_iota(jnp.int32, shape, 0) == me * own + lax.broadcasted_iota(jnp.int32, shape, 1)
    loss_ref[...] = jnp.sum(jnp.where(mine, to_column(loss), 0.0), axis=0, keepdims=True)[:, :own]

    @pl.loop(0, chunks)
    def _(c):
        span = span_of(c)
        g = lax.dot_general(
            delta[:, span], s_all[...], (((0,), (0,)), ((), ())), preferred_element_type=jnp.float32
        )
        x = sw_raw[span].astype(jnp.float32)
        inverse = jnp.concatenate([sw_inv[span]] * (width // LANES), axis=1)
        projected = jnp.sum(x * g, axis=1, keepdims=True)
        pgrad_ref[span] = inverse * g - x * ((inverse * inverse * inverse) * projected)

    whole(3, landed).wait_recv()
    g = jnp.sum(landed[...], axis=0)
    projected = jnp.sum(s_own * g, axis=1, keepdims=True)
    sgrad_ref[...] = s_own_inv * g - s_own * (s_own_inv * s_own_inv * s_own_inv) * projected
    for phase, target in enumerate((rows_buf, sums1, sums2, landed)):
        whole(phase, target).wait_send()


def body(dp, proto, teacher_rows, student_rows, teacher_protos, student_protos):
    n = dp * proto
    own, width = teacher_rows.shape
    count = teacher_protos.shape[0]
    rows = n * own
    cols = min(count, max(LANES, 32768 // rows))
    f32, bf16 = jnp.float32, jnp.bfloat16
    vmem = pl.BlockSpec(memory_space=pltpu.VMEM)
    hbm = pl.BlockSpec(memory_space=pl.ANY)
    loss, sgrad, pgrad = pl.pallas_call(
        functools.partial(kernel, dp, proto, cols),
        out_shape=(
            jax.ShapeDtypeStruct((1, own), f32),
            jax.ShapeDtypeStruct((own, width), f32),
            jax.ShapeDtypeStruct((count, width), f32),
        ),
        in_specs=[vmem, vmem, hbm, hbm],
        out_specs=(vmem, vmem, vmem),
        scratch_shapes=[
            pltpu.VMEM((count, width), bf16),
            pltpu.VMEM((count, width), bf16),
            pltpu.VMEM((count, width), bf16),
            pltpu.VMEM((count, width), bf16),
            pltpu.VMEM((count, LANES), f32),
            pltpu.VMEM((rows, count), f32),
            pltpu.VMEM((rows, count), f32),
            pltpu.VMEM((rows, count), bf16),
            pltpu.VMEM((n, 2 * own, width), f32),
            pltpu.VMEM((n, 2, rows), f32),
            pltpu.VMEM((n, 2, rows), f32),
            pltpu.VMEM((n, own, width), f32),
            pltpu.VMEM((n, own, width), f32),
            pltpu.VMEM((rows, width), bf16),
            pltpu.VMEM((rows, width), bf16),
            pltpu.VMEM((1, count), f32),
            pltpu.SemaphoreType.DMA((2, LOAD_PARTS)),
            pltpu.SemaphoreType.DMA((4,)),
            pltpu.SemaphoreType.DMA((4,)),
        ],
        compiler_params=pltpu.CompilerParams(
            collective_id=0, has_side_effects=True, vmem_limit_bytes=56 * 1024 * 1024
        ),
    )(teacher_rows, student_rows, teacher_protos, student_protos)
    return loss.reshape(own), sgrad, pgrad


def solution(mesh):
    spec = P(AXES, None)
    return jax.shard_map(
        functools.partial(body, mesh.shape["dp"], mesh.shape["proto"]),
        mesh=mesh,
        in_specs=(spec,) * 4,
        out_specs=(P(AXES), spec, spec),
        check_vma=False,
    )
```

```python
import functools

import jax
import jax.numpy as jnp
from jax import lax
from jax.experimental import pallas as pl
from jax.experimental.pallas import tpu as pltpu
from jax.sharding import PartitionSpec as P

TEACH_TEMP = 0.04
STUD_TEMP = 0.1
LOSS_SCALE = 4096.0
EPSILON = 1e-06
AXES = ("dp", "proto")
LANES = 128
LOAD_PARTS = 4


def inverse_norm(x):
    return lax.rsqrt(jnp.sum(x * x, axis=-1, keepdims=True) + EPSILON)


def sum_wide(x):
    ones = jnp.ones((x.shape[1], LANES), jnp.bfloat16)
    high = x.astype(jnp.bfloat16)
    low = (x - high.astype(jnp.float32)).astype(jnp.bfloat16)
    return jnp.dot(high, ones, preferred_element_type=jnp.float32) + jnp.dot(
        low, ones, preferred_element_type=jnp.float32
    )


def widen(x, width):
    return jnp.concatenate([x] * (width // LANES), axis=1)


def fold_lanes(x):
    total = x[:, :LANES]
    for start in range(LANES, x.shape[1], LANES):
        total = total + x[:, start:start + LANES]
    return total


def eye():
    shape = (LANES, LANES)
    return lax.broadcasted_iota(jnp.int32, shape, 0) == lax.broadcasted_iota(jnp.int32, shape, 1)


def to_lanes(column):
    blocks = [
        jnp.sum(jnp.where(eye(), column[i:i + LANES], 0.0), axis=0, keepdims=True)
        for i in range(0, column.shape[0], LANES)
    ]
    return blocks[0] if len(blocks) == 1 else jnp.concatenate(blocks, axis=1)


def to_column(row):
    blocks = [
        jnp.sum(jnp.where(eye(), row[:, i:i + LANES], 0.0), axis=1, keepdims=True)
        for i in range(0, row.shape[1], LANES)
    ]
    return blocks[0] if len(blocks) == 1 else jnp.concatenate(blocks, axis=0)


def kernel(
    dp, proto, cols,
    t_ref, s_ref, tw_hbm, sw_hbm,
    loss_ref, sgrad_ref, pgrad_ref,
    tw_raw, sw_raw, tw_unit, sw_unit, sw_inv, texp, logit, delta,
    rows_buf, sums1, sums2, part, landed, t_all, s_all,
    load_sem, send_sem, recv_sem,
):
    n = dp * proto
    own = t_ref.shape[0]
    total_rows = n * own
    width = t_ref.shape[1]
    count = tw_raw.shape[0]
    chunks = count // cols
    me = lax.axis_index("dp") * proto + lax.axis_index("proto")

    def coords(j):
        peer = lax.rem(me + j, n)
        return peer, (lax.div(peer, proto), lax.rem(peer, proto))

    piece = count // LOAD_PARTS
    loads = []
    for k in range(LOAD_PARTS):
        for index, (hbm, raw) in enumerate(((tw_hbm, tw_raw), (sw_hbm, sw_raw))):
            span = pl.ds(k * piece, piece)
            copy = pltpu.make_async_copy(hbm.at[span], raw.at[span], load_sem.at[index, k])
            copy.start()
            loads.append(copy)

    barrier = pltpu.get_barrier_semaphore()

    @pl.loop(1, n)
    def _(j):
        pl.semaphore_signal(barrier, inc=1, device_id=coords(j)[1], device_id_type=pl.DeviceIdType.MESH)

    t_own = t_ref[...].astype(jnp.float32)
    s_own = s_ref[...].astype(jnp.float32)
    s_own_inv = inverse_norm(s_own)
    t_rounded = (t_own * inverse_norm(t_own)).astype(jnp.bfloat16).astype(jnp.float32)
    s_rounded = (s_own * s_own_inv).astype(jnp.bfloat16).astype(jnp.float32)
    rows_buf[me] = jnp.concatenate([t_rounded, s_rounded], axis=0)
    pl.semaphore_wait(barrier, n - 1)

    def spread(phase, source, target):
        @pl.loop(1, n)
        def _(j):
            peer, device = coords(j)
            pltpu.make_async_remote_copy(
                src_ref=source(peer), dst_ref=target.at[me],
                send_sem=send_sem.at[phase], recv_sem=recv_sem.at[phase],
                device_id=device, device_id_type=pl.DeviceIdType.MESH,
            ).start()

    def whole(phase, target):
        span = pl.ds(0, n - 1)
        return pltpu.make_async_remote_copy(
            src_ref=target.at[span], dst_ref=target.at[span],
            send_sem=send_sem.at[phase], recv_sem=recv_sem.at[phase],
            device_id=coords(1)[1], device_id_type=pl.DeviceIdType.MESH,
        )

    spread(0, lambda peer: rows_buf.at[me], rows_buf)

    norm_rows = min(piece, 512)
    for k in range(LOAD_PARTS):
        for index, raw in enumerate((tw_raw, sw_raw)):
            loads[2 * k + index].wait()

            @pl.loop(0, piece // norm_rows)
            def _(c, k=k, index=index, raw=raw):
                span = pl.ds(pl.multiple_of(k * piece + c * norm_rows, norm_rows), norm_rows)
                x = raw[span].astype(jnp.float32)
                inverse = lax.rsqrt(sum_wide(x * x) + EPSILON)
                unit = (x * widen(inverse, width)).astype(jnp.bfloat16)
                if index == 0:
                    tw_unit[span] = unit
                else:
                    sw_unit[span] = unit
                    sw_inv[span] = inverse

    whole(0, rows_buf).wait_recv()
    paired = rows_buf[...].reshape(n // 2, 2, 2 * own, width)
    first, second = paired[:, 0], paired[:, 1]
    upper = lax.broadcasted_iota(jnp.int32, first.shape, 1) < own
    t_all[...] = jnp.where(upper, first, pltpu.roll(second, own, 1)).reshape(total_rows, width).astype(jnp.bfloat16)
    s_all[...] = jnp.where(upper, pltpu.roll(first, own, 1), second).reshape(total_rows, width).astype(jnp.bfloat16)

    transposed = (((1,), (1,)), ((), ()))
    zeros = jnp.zeros((total_rows, LANES), jnp.float32)

    def span_of(c):
        return pl.ds(pl.multiple_of(c * cols, cols), cols)

    def first_pass(c, carry):
        row_sum, exp_sum = carry
        span = span_of(c)
        expo = jnp.exp(
            lax.dot_general(t_all[...], tw_unit[span], transposed, preferred_element_type=jnp.float32)
            * (1.0 / TEACH_TEMP)
        )
        texp[:, span] = expo
        scale = 1.0 / jnp.sum(expo, axis=0, keepdims=True)
        row_sum = row_sum + fold_lanes(expo * scale)
        logits = lax.dot_general(
            s_all[...], sw_unit[span], transposed, preferred_element_type=jnp.float32
        ) * (1.0 / STUD_TEMP)
        logit[:, span] = logits
        exp_sum = exp_sum + fold_lanes(jnp.exp(logits))
        return row_sum, exp_sum

    def share(phase, sums, one, two):
        sums[me] = jnp.concatenate(
            [to_lanes(jnp.sum(x, axis=1, keepdims=True)) for x in (one, two)], axis=0
        )
        spread(phase, lambda peer: sums.at[me], sums)
        whole(phase, sums).wait_recv()
        total = jnp.sum(sums[...], axis=0)
        return total[0:1], total[1:2]

    row_sum, exp_sum = lax.fori_loop(0, chunks, first_pass, (zeros, zeros))
    row_total, exp_total = share(1, sums1, row_sum, exp_sum)
    row_scale = to_column(1.0 / row_total)

    def second_pass(c, carry):
        row_sum, dot_sum = carry
        span = span_of(c)
        expo = texp[:, span]
        scale = 1.0 / jnp.sum(expo * row_scale, axis=0, keepdims=True)
        scaled = expo * scale
        texp[:, span] = scaled
        return row_sum + fold_lanes(scaled), dot_sum + fold_lanes(scaled * logit[:, span])

    row_sum, dot_sum = lax.fori_loop(0, chunks, second_pass, (zeros, zeros))
    row_total, dot_total = share(2, sums2, row_sum, dot_sum)
    factor = LOSS_SCALE / STUD_TEMP
    row_scale = to_column(factor / row_total)
    exp_scale = to_column(factor / exp_total)

    def third_pass(c, carry):
        span = span_of(c)
        gradient = (jnp.exp(logit[:, span]) * exp_scale - texp[:, span] * row_scale).astype(jnp.bfloat16)
        delta[:, span] = gradient
        return carry + jnp.dot(gradient, sw_unit[span], preferred_element_type=jnp.float32)

    row_part = lax.fori_loop(0, chunks, third_pass, jnp.zeros((total_rows, width), jnp.float32))
    part[...] = row_part.reshape(n, own, width)
    landed[me] = part[me]
    spread(3, lambda peer: part.at[peer], landed)

    loss = jnp.log(exp_total) - dot_total / row_total
    shape = (total_rows, LANES)
    mine = lax.broadcasted_iota(jnp.int32, shape, 0) == me * own + lax.broadcasted_iota(jnp.int32, shape, 1)
    loss_ref[...] = jnp.sum(jnp.where(mine, to_column(loss), 0.0), axis=0, keepdims=True)[:, :own]

    @pl.loop(0, chunks)
    def _(c):
        span = span_of(c)
        g = lax.dot_general(
            delta[:, span], s_all[...], (((0,), (0,)), ((), ())), preferred_element_type=jnp.float32
        )
        x = sw_raw[span].astype(jnp.float32)
        inverse = sw_inv[span]
        pull = (inverse * inverse * inverse) * sum_wide(x * g)
        pgrad_ref[span] = widen(inverse, width) * g - x * widen(pull, width)

    whole(3, landed).wait_recv()
    g = jnp.sum(landed[...], axis=0)
    projected = jnp.sum(s_own * g, axis=1, keepdims=True)
    sgrad_ref[...] = s_own_inv * g - s_own * (s_own_inv * s_own_inv * s_own_inv) * projected
    for phase, target in enumerate((rows_buf, sums1, sums2, landed)):
        whole(phase, target).wait_send()


def body(dp, proto, teacher_rows, student_rows, teacher_protos, student_protos):
    n = dp * proto
    own, width = teacher_rows.shape
    count = teacher_protos.shape[0]
    rows = n * own
    cols = min(count, max(LANES, 65536 // rows))
    f32, bf16 = jnp.float32, jnp.bfloat16
    vmem = pl.BlockSpec(memory_space=pltpu.VMEM)
    hbm = pl.BlockSpec(memory_space=pl.ANY)
    loss, sgrad, pgrad = pl.pallas_call(
        functools.partial(kernel, dp, proto, cols),
        out_shape=(
            jax.ShapeDtypeStruct((1, own), f32),
            jax.ShapeDtypeStruct((own, width), f32),
            pltpu.VMEM((count, width), f32),
        ),
        in_specs=[vmem, vmem, hbm, hbm],
        out_specs=(vmem, vmem, vmem),
        scratch_shapes=[
            pltpu.VMEM((count, width), bf16),
            pltpu.VMEM((count, width), bf16),
            pltpu.VMEM((count, width), bf16),
            pltpu.VMEM((count, width), bf16),
            pltpu.VMEM((count, LANES), f32),
            pltpu.VMEM((rows, count), f32),
            pltpu.VMEM((rows, count), f32),
            pltpu.VMEM((rows, count), bf16),
            pltpu.VMEM((n, 2 * own, width), f32),
            pltpu.VMEM((n, 2, rows), f32),
            pltpu.VMEM((n, 2, rows), f32),
            pltpu.VMEM((n, own, width), f32),
            pltpu.VMEM((n, own, width), f32),
            pltpu.VMEM((rows, width), bf16),
            pltpu.VMEM((rows, width), bf16),
            pltpu.SemaphoreType.DMA((2, LOAD_PARTS)),
            pltpu.SemaphoreType.DMA((4,)),
            pltpu.SemaphoreType.DMA((4,)),
        ],
        compiler_params=pltpu.CompilerParams(
            collective_id=0, has_side_effects=True, vmem_limit_bytes=56 * 1024 * 1024
        ),
    )(teacher_rows, student_rows, teacher_protos, student_protos)
    return loss.reshape(own), sgrad, pgrad


def solution(mesh):
    spec = P(AXES, None)
    return jax.shard_map(
        functools.partial(body, mesh.shape["dp"], mesh.shape["proto"]),
        mesh=mesh,
        in_specs=(spec,) * 4,
        out_specs=(P(AXES), spec, spec),
        check_vma=False,
    )
```

```python
import functools

import jax
import jax.numpy as jnp
from jax import lax
from jax.experimental import pallas as pl
from jax.experimental.pallas import tpu as pltpu
from jax.sharding import PartitionSpec as P

TEACH_TEMP = 0.04
STUD_TEMP = 0.1
LOSS_SCALE = 4096.0
EPSILON = 1e-06
AXES = ("dp", "proto")
LANES = 128
LOAD_PARTS = 4


def inverse_norm(x):
    return lax.rsqrt(jnp.sum(x * x, axis=-1, keepdims=True) + EPSILON)


def sum_wide(x):
    ones = jnp.ones((x.shape[1], LANES), jnp.bfloat16)
    high = x.astype(jnp.bfloat16)
    low = (x - high.astype(jnp.float32)).astype(jnp.bfloat16)
    return jnp.dot(high, ones, preferred_element_type=jnp.float32) + jnp.dot(
        low, ones, preferred_element_type=jnp.float32
    )


def widen(x, width):
    return jnp.concatenate([x] * (width // LANES), axis=1)


def fold_lanes(x):
    total = x[:, :LANES]
    for start in range(LANES, x.shape[1], LANES):
        total = total + x[:, start:start + LANES]
    return total


def eye():
    shape = (LANES, LANES)
    return lax.broadcasted_iota(jnp.int32, shape, 0) == lax.broadcasted_iota(jnp.int32, shape, 1)


def to_lanes(column):
    blocks = [
        jnp.sum(jnp.where(eye(), column[i:i + LANES], 0.0), axis=0, keepdims=True)
        for i in range(0, column.shape[0], LANES)
    ]
    return blocks[0] if len(blocks) == 1 else jnp.concatenate(blocks, axis=1)


def to_column(row):
    blocks = [
        jnp.sum(jnp.where(eye(), row[:, i:i + LANES], 0.0), axis=1, keepdims=True)
        for i in range(0, row.shape[1], LANES)
    ]
    return blocks[0] if len(blocks) == 1 else jnp.concatenate(blocks, axis=0)


def kernel(
    dp, proto, cols,
    t_ref, s_ref, tw_hbm, sw_hbm,
    loss_ref, sgrad_ref, pgrad_ref,
    tw_raw, sw_raw, tw_unit, sw_unit, sw_inv, texp, logit, sexp, delta,
    rows_buf, sums1, sums2, part, landed, t_all, s_all,
    load_sem, send_sem, recv_sem,
):
    n = dp * proto
    own = t_ref.shape[0]
    total_rows = n * own
    width = t_ref.shape[1]
    count = tw_raw.shape[0]
    chunks = count // cols
    me = lax.axis_index("dp") * proto + lax.axis_index("proto")

    def coords(j):
        peer = lax.rem(me + j, n)
        return peer, (lax.div(peer, proto), lax.rem(peer, proto))

    piece = count // LOAD_PARTS
    loads = []
    for k in range(LOAD_PARTS):
        for index, (hbm, raw) in enumerate(((tw_hbm, tw_raw), (sw_hbm, sw_raw))):
            span = pl.ds(k * piece, piece)
            copy = pltpu.make_async_copy(hbm.at[span], raw.at[span], load_sem.at[index, k])
            copy.start()
            loads.append(copy)

    barrier = pltpu.get_barrier_semaphore()

    @pl.loop(1, n)
    def _(j):
        pl.semaphore_signal(barrier, inc=1, device_id=coords(j)[1], device_id_type=pl.DeviceIdType.MESH)

    t_own = t_ref[...].astype(jnp.float32)
    s_own = s_ref[...].astype(jnp.float32)
    s_own_inv = inverse_norm(s_own)
    t_rounded = (t_own * inverse_norm(t_own)).astype(jnp.bfloat16).astype(jnp.float32)
    s_rounded = (s_own * s_own_inv).astype(jnp.bfloat16).astype(jnp.float32)
    rows_buf[me] = jnp.concatenate([t_rounded, s_rounded], axis=0)
    pl.semaphore_wait(barrier, n - 1)

    def spread(phase, source, target):
        @pl.loop(1, n)
        def _(j):
            peer, device = coords(j)
            pltpu.make_async_remote_copy(
                src_ref=source(peer), dst_ref=target.at[me],
                send_sem=send_sem.at[phase], recv_sem=recv_sem.at[phase],
                device_id=device, device_id_type=pl.DeviceIdType.MESH,
            ).start()

    def whole(phase, target):
        span = pl.ds(0, n - 1)
        return pltpu.make_async_remote_copy(
            src_ref=target.at[span], dst_ref=target.at[span],
            send_sem=send_sem.at[phase], recv_sem=recv_sem.at[phase],
            device_id=coords(1)[1], device_id_type=pl.DeviceIdType.MESH,
        )

    spread(0, lambda peer: rows_buf.at[me], rows_buf)

    norm_rows = min(piece, 512)
    for k in range(LOAD_PARTS):
        for index, raw in enumerate((tw_raw, sw_raw)):
            loads[2 * k + index].wait()

            @pl.loop(0, piece // norm_rows)
            def _(c, k=k, index=index, raw=raw):
                span = pl.ds(pl.multiple_of(k * piece + c * norm_rows, norm_rows), norm_rows)
                x = raw[span].astype(jnp.float32)
                inverse = lax.rsqrt(sum_wide(x * x) + EPSILON)
                unit = (x * widen(inverse, width)).astype(jnp.bfloat16)
                if index == 0:
                    tw_unit[span] = unit
                else:
                    sw_unit[span] = unit
                    sw_inv[span] = inverse

    whole(0, rows_buf).wait_recv()
    paired = rows_buf[...].reshape(n // 2, 2, 2 * own, width)
    first, second = paired[:, 0], paired[:, 1]
    upper = lax.broadcasted_iota(jnp.int32, first.shape, 1) < own
    t_all[...] = jnp.where(upper, first, pltpu.roll(second, own, 1)).reshape(total_rows, width).astype(jnp.bfloat16)
    s_all[...] = jnp.where(upper, pltpu.roll(first, own, 1), second).reshape(total_rows, width).astype(jnp.bfloat16)

    transposed = (((1,), (1,)), ((), ()))
    zeros = jnp.zeros((total_rows, LANES), jnp.float32)

    def span_of(c):
        return pl.ds(c * cols, cols)

    def over_chunks(step, carry):
        for c in range(chunks):
            carry = step(c, carry)
        return carry

    def first_pass(c, carry):
        span = span_of(c)
        expo = jnp.exp(
            lax.dot_general(t_all[...], tw_unit[span], transposed, preferred_element_type=jnp.float32)
            * (1.0 / TEACH_TEMP)
        )
        texp[:, span] = expo
        scale = 1.0 / jnp.sum(expo, axis=0, keepdims=True)
        return carry + fold_lanes(expo * scale)

    def student_pass(c, carry):
        span = span_of(c)
        logits = lax.dot_general(
            s_all[...], sw_unit[span], transposed, preferred_element_type=jnp.float32
        ) * (1.0 / STUD_TEMP)
        logit[:, span] = logits
        expo = jnp.exp(logits)
        sexp[:, span] = expo
        return carry + fold_lanes(expo)

    def send_sums(phase, sums, parts):
        rows = [to_lanes(jnp.sum(x, axis=1, keepdims=True)) for x in parts]
        sums[me] = rows[0] if len(rows) == 1 else jnp.concatenate(rows, axis=0)
        spread(phase, lambda peer: sums.at[me], sums)

    def receive_sums(phase, sums):
        whole(phase, sums).wait_recv()
        return jnp.sum(sums[...], axis=0)

    send_sums(1, sums1, (over_chunks(first_pass, zeros),))
    exp_sum = over_chunks(student_pass, zeros)
    row_total = receive_sums(1, sums1)
    row_scale = to_column(1.0 / row_total)

    def second_pass(c, carry):
        row_sum, dot_sum = carry
        span = span_of(c)
        expo = texp[:, span]
        scale = 1.0 / jnp.sum(expo * row_scale, axis=0, keepdims=True)
        scaled = expo * scale
        texp[:, span] = scaled
        return row_sum + fold_lanes(scaled), dot_sum + fold_lanes(scaled * logit[:, span])

    row_sum, dot_sum = over_chunks(second_pass, (zeros, zeros))
    send_sums(2, sums2, (row_sum, dot_sum, exp_sum))
    total = receive_sums(2, sums2)
    row_total, dot_total, exp_total = total[0:1], total[1:2], total[2:3]
    factor = LOSS_SCALE / STUD_TEMP
    row_scale = to_column(factor / row_total)
    exp_scale = to_column(factor / exp_total)

    def third_pass(c, carry):
        span = span_of(c)
        gradient = (sexp[:, span] * exp_scale - texp[:, span] * row_scale).astype(jnp.bfloat16)
        delta[:, span] = gradient
        return carry + jnp.dot(gradient, sw_unit[span], preferred_element_type=jnp.float32)

    row_part = over_chunks(third_pass, jnp.zeros((total_rows, width), jnp.float32))
    part[...] = row_part.reshape(n, own, width)
    landed[me] = part[me]
    spread(3, lambda peer: part.at[peer], landed)

    loss = jnp.log(exp_total) - dot_total / row_total
    shape = (total_rows, LANES)
    mine = lax.broadcasted_iota(jnp.int32, shape, 0) == me * own + lax.broadcasted_iota(jnp.int32, shape, 1)
    loss_ref[...] = jnp.sum(jnp.where(mine, to_column(loss), 0.0), axis=0, keepdims=True)[:, :own]

    for c in range(chunks):
        span = span_of(c)
        g = lax.dot_general(
            delta[:, span], s_all[...], (((0,), (0,)), ((), ())), preferred_element_type=jnp.float32
        )
        x = sw_raw[span].astype(jnp.float32)
        inverse = sw_inv[span]
        pull = (inverse * inverse * inverse) * sum_wide(x * g)
        pgrad_ref[span] = widen(inverse, width) * g - x * widen(pull, width)

    whole(3, landed).wait_recv()
    g = jnp.sum(landed[...], axis=0)
    projected = jnp.sum(s_own * g, axis=1, keepdims=True)
    sgrad_ref[...] = s_own_inv * g - s_own * (s_own_inv * s_own_inv * s_own_inv) * projected
    for phase, target in enumerate((rows_buf, sums1, sums2, landed)):
        whole(phase, target).wait_send()


def body(dp, proto, teacher_rows, student_rows, teacher_protos, student_protos):
    n = dp * proto
    own, width = teacher_rows.shape
    count = teacher_protos.shape[0]
    rows = n * own
    cols = min(count, max(LANES, 65536 // rows))
    f32, bf16 = jnp.float32, jnp.bfloat16
    vmem = pl.BlockSpec(memory_space=pltpu.VMEM)
    hbm = pl.BlockSpec(memory_space=pl.ANY)
    loss, sgrad, pgrad = pl.pallas_call(
        functools.partial(kernel, dp, proto, cols),
        out_shape=(
            jax.ShapeDtypeStruct((1, own), f32),
            jax.ShapeDtypeStruct((own, width), f32),
            pltpu.VMEM((count, width), f32),
        ),
        in_specs=[vmem, vmem, hbm, hbm],
        out_specs=(vmem, vmem, vmem),
        scratch_shapes=[
            pltpu.VMEM((count, width), bf16),
            pltpu.VMEM((count, width), bf16),
            pltpu.VMEM((count, width), bf16),
            pltpu.VMEM((count, width), bf16),
            pltpu.VMEM((count, LANES), f32),
            pltpu.VMEM((rows, count), f32),
            pltpu.VMEM((rows, count), f32),
            pltpu.VMEM((rows, count), f32),
            pltpu.VMEM((rows, count), bf16),
            pltpu.VMEM((n, 2 * own, width), f32),
            pltpu.VMEM((n, 1, rows), f32),
            pltpu.VMEM((n, 3, rows), f32),
            pltpu.VMEM((n, own, width), f32),
            pltpu.VMEM((n, own, width), f32),
            pltpu.VMEM((rows, width), bf16),
            pltpu.VMEM((rows, width), bf16),
            pltpu.SemaphoreType.DMA((2, LOAD_PARTS)),
            pltpu.SemaphoreType.DMA((4,)),
            pltpu.SemaphoreType.DMA((4,)),
        ],
        compiler_params=pltpu.CompilerParams(
            collective_id=0, has_side_effects=True, vmem_limit_bytes=56 * 1024 * 1024
        ),
    )(teacher_rows, student_rows, teacher_protos, student_protos)
    return loss.reshape(own), sgrad, pgrad


def solution(mesh):
    spec = P(AXES, None)
    return jax.shard_map(
        functools.partial(body, mesh.shape["dp"], mesh.shape["proto"]),
        mesh=mesh,
        in_specs=(spec,) * 4,
        out_specs=(P(AXES), spec, spec),
        check_vma=False,
    )
```

```python
import functools

import jax
import jax.numpy as jnp
from jax import lax
from jax.experimental import pallas as pl
from jax.experimental.pallas import tpu as pltpu
from jax.sharding import PartitionSpec as P

TEACH_TEMP = 0.04
STUD_TEMP = 0.1
LOSS_SCALE = 4096.0
EPSILON = 1e-06
AXES = ("dp", "proto")
LANES = 128
LOAD_PARTS = 4


def inner_size(n):
    size = 1
    while n % (2 * size) == 0 and 2 * size * size <= n:
        size *= 2
    return size


def inverse_norm(x):
    return lax.rsqrt(jnp.sum(x * x, axis=-1, keepdims=True) + EPSILON)


def sum_wide(x):
    ones = jnp.ones((x.shape[1], LANES), jnp.bfloat16)
    high = x.astype(jnp.bfloat16)
    low = (x - high.astype(jnp.float32)).astype(jnp.bfloat16)
    return jnp.dot(high, ones, preferred_element_type=jnp.float32) + jnp.dot(
        low, ones, preferred_element_type=jnp.float32
    )


def widen(x, width):
    return jnp.concatenate([x] * (width // LANES), axis=1)


def fold_lanes(x):
    total = x[:, :LANES]
    for start in range(LANES, x.shape[1], LANES):
        total = total + x[:, start:start + LANES]
    return total


def eye():
    shape = (LANES, LANES)
    return lax.broadcasted_iota(jnp.int32, shape, 0) == lax.broadcasted_iota(jnp.int32, shape, 1)


def to_lanes(column):
    blocks = [
        jnp.sum(jnp.where(eye(), column[i:i + LANES], 0.0), axis=0, keepdims=True)
        for i in range(0, column.shape[0], LANES)
    ]
    return blocks[0] if len(blocks) == 1 else jnp.concatenate(blocks, axis=1)


def to_column(row):
    blocks = [
        jnp.sum(jnp.where(eye(), row[:, i:i + LANES], 0.0), axis=1, keepdims=True)
        for i in range(0, row.shape[1], LANES)
    ]
    return blocks[0] if len(blocks) == 1 else jnp.concatenate(blocks, axis=0)


def kernel(
    dp, proto, cols,
    t_ref, s_ref, tw_hbm, sw_hbm,
    loss_ref, sgrad_ref, pgrad_ref,
    tw_raw, sw_raw, tw_unit, sw_unit, sw_inv, texp, logit, sexp, delta,
    rows_buf, sums1, again1, sums2, again2, part, landed, passed, summed, t_all, s_all,
    load_sem, send_sem, recv_sem,
):
    n = dp * proto
    own = t_ref.shape[0]
    total_rows = n * own
    width = t_ref.shape[1]
    count = tw_raw.shape[0]
    chunks = count // cols
    me = lax.axis_index("dp") * proto + lax.axis_index("proto")

    inner = inner_size(n)
    outer = n // inner
    low, high = lax.rem(me, inner), lax.div(me, inner)
    sizes, places = (inner, outer), (low, high)

    def neighbour(stage, j):
        place = lax.rem(places[stage] + j, sizes[stage])
        peer = high * inner + place if stage == 0 else place * inner + low
        return place, (lax.div(peer, proto), lax.rem(peer, proto))

    piece = count // LOAD_PARTS
    loads = []
    for index, (hbm, raw) in enumerate(((tw_hbm, tw_raw), (sw_hbm, sw_raw))):
        for k in range(LOAD_PARTS):
            span = pl.ds(k * piece, piece)
            copy = pltpu.make_async_copy(hbm.at[span], raw.at[span], load_sem.at[index, k])
            copy.start()
            loads.append(copy)

    barrier = pltpu.get_barrier_semaphore()

    for stage in range(2):
        for j in range(1, sizes[stage]):
            pl.semaphore_signal(
                barrier, inc=1, device_id=neighbour(stage, j)[1], device_id_type=pl.DeviceIdType.MESH
            )

    t_own = t_ref[...].astype(jnp.float32)
    s_own = s_ref[...].astype(jnp.float32)
    s_own_inv = inverse_norm(s_own)
    t_rounded = (t_own * inverse_norm(t_own)).astype(jnp.bfloat16).astype(jnp.float32)
    s_rounded = (s_own * s_own_inv).astype(jnp.bfloat16).astype(jnp.float32)
    rows_buf[high, low] = jnp.concatenate([t_rounded, s_rounded], axis=0)
    pl.semaphore_wait(barrier, inner + outer - 2)

    def spread(phase, stage, source, target):
        for j in range(1, sizes[stage]):
            place, device = neighbour(stage, j)
            pltpu.make_async_remote_copy(
                src_ref=source(place), dst_ref=target,
                send_sem=send_sem.at[phase, stage], recv_sem=recv_sem.at[phase, stage],
                device_id=device, device_id_type=pl.DeviceIdType.MESH,
            ).start()

    def whole(phase, stage, view):
        return pltpu.make_async_remote_copy(
            src_ref=view, dst_ref=view,
            send_sem=send_sem.at[phase, stage], recv_sem=recv_sem.at[phase, stage],
            device_id=neighbour(stage, 1)[1], device_id_type=pl.DeviceIdType.MESH,
        )

    def others(stage, buffer):
        return buffer.at[pl.ds(0, sizes[stage] - 1)]

    block_rows = rows_buf.at[high]
    spread(0, 0, lambda place: block_rows.at[low], block_rows.at[low])

    norm_rows = min(piece, 512)
    for index, raw in enumerate((tw_raw, sw_raw)):
        if index == 1:
            whole(0, 0, others(0, block_rows)).wait_recv()
            spread(0, 1, lambda place: block_rows, block_rows)
        for k in range(LOAD_PARTS):
            loads[index * LOAD_PARTS + k].wait()

            @pl.loop(0, piece // norm_rows)
            def _(c, k=k, index=index, raw=raw):
                span = pl.ds(pl.multiple_of(k * piece + c * norm_rows, norm_rows), norm_rows)
                x = raw[span].astype(jnp.float32)
                inverse = lax.rsqrt(sum_wide(x * x) + EPSILON)
                unit = (x * widen(inverse, width)).astype(jnp.bfloat16)
                if index == 0:
                    tw_unit[span] = unit
                else:
                    sw_unit[span] = unit
                    sw_inv[span] = inverse

    whole(0, 1, others(1, rows_buf)).wait_recv()
    paired = rows_buf[...].reshape(n // 2, 2, 2 * own, width)
    first, second = paired[:, 0], paired[:, 1]
    upper = lax.broadcasted_iota(jnp.int32, first.shape, 1) < own
    t_all[...] = jnp.where(upper, first, pltpu.roll(second, own, 1)).reshape(total_rows, width).astype(jnp.bfloat16)
    s_all[...] = jnp.where(upper, pltpu.roll(first, own, 1), second).reshape(total_rows, width).astype(jnp.bfloat16)

    transposed = (((1,), (1,)), ((), ()))
    zeros = jnp.zeros((total_rows, LANES), jnp.float32)

    def span_of(c):
        return pl.ds(c * cols, cols)

    half = (chunks + 1) // 2

    def over_chunks(step, carry, first=0, last=chunks):
        for c in range(first, last):
            carry = step(c, carry)
        return carry

    def first_pass(c, carry):
        span = span_of(c)
        expo = jnp.exp(
            lax.dot_general(t_all[...], tw_unit[span], transposed, preferred_element_type=jnp.float32)
            * (1.0 / TEACH_TEMP)
        )
        texp[:, span] = expo
        scale = 1.0 / jnp.sum(expo, axis=0, keepdims=True)
        return carry + fold_lanes(expo * scale)

    def student_pass(c, carry):
        span = span_of(c)
        logits = lax.dot_general(
            s_all[...], sw_unit[span], transposed, preferred_element_type=jnp.float32
        ) * (1.0 / STUD_TEMP)
        logit[:, span] = logits
        expo = jnp.exp(logits)
        sexp[:, span] = expo
        return carry + fold_lanes(expo)

    def send_sums(phase, sums, parts):
        rows = [to_lanes(jnp.sum(x, axis=1, keepdims=True)) for x in parts]
        sums[low] = rows[0] if len(rows) == 1 else jnp.concatenate(rows, axis=0)
        spread(phase, 0, lambda place: sums.at[low], sums.at[low])

    def pass_on(phase, sums, again):
        whole(phase, 0, others(0, sums)).wait_recv()
        again[high] = jnp.sum(sums[...], axis=0)
        spread(phase, 1, lambda place: again.at[high], again.at[high])

    def receive_sums(phase, again):
        whole(phase, 1, others(1, again)).wait_recv()
        return jnp.sum(again[...], axis=0)

    send_sums(1, sums1, (over_chunks(first_pass, zeros),))
    exp_sum = over_chunks(student_pass, zeros, 0, half)
    pass_on(1, sums1, again1)
    exp_sum = over_chunks(student_pass, exp_sum, half, chunks)
    row_total = receive_sums(1, again1)
    row_scale = to_column(1.0 / row_total)

    def second_pass(c, carry):
        row_sum, dot_sum = carry
        span = span_of(c)
        expo = texp[:, span]
        scale = 1.0 / jnp.sum(expo * row_scale, axis=0, keepdims=True)
        scaled = expo * scale
        texp[:, span] = scaled
        return row_sum + fold_lanes(scaled), dot_sum + fold_lanes(scaled * logit[:, span])

    row_sum, dot_sum = over_chunks(second_pass, (zeros, zeros))
    send_sums(2, sums2, (row_sum, dot_sum, exp_sum))
    pass_on(2, sums2, again2)
    total = receive_sums(2, again2)
    row_total, dot_total, exp_total = total[0:1], total[1:2], total[2:3]
    factor = LOSS_SCALE / STUD_TEMP
    row_scale = to_column(factor / row_total)
    exp_scale = to_column(factor / exp_total)

    def third_pass(c, carry):
        span = span_of(c)
        gradient = (sexp[:, span] * exp_scale - texp[:, span] * row_scale).astype(jnp.bfloat16)
        delta[:, span] = gradient
        return carry + jnp.dot(gradient, sw_unit[span], preferred_element_type=jnp.float32)

    row_part = over_chunks(third_pass, jnp.zeros((total_rows, width), jnp.float32))
    blocks = row_part.reshape(outer, inner, own, width)
    for h in range(outer):
        part[:, h] = blocks[h]
    landed[low] = part[low]
    spread(3, 0, lambda place: part.at[place], landed.at[low])

    loss = jnp.log(exp_total) - dot_total / row_total
    shape = (total_rows, LANES)
    mine = lax.broadcasted_iota(jnp.int32, shape, 0) == me * own + lax.broadcasted_iota(jnp.int32, shape, 1)
    loss_ref[...] = jnp.sum(jnp.where(mine, to_column(loss), 0.0), axis=0, keepdims=True)[:, :own]

    def grad_pass(c, carry):
        span = span_of(c)
        g = lax.dot_general(
            delta[:, span], s_all[...], (((0,), (0,)), ((), ())), preferred_element_type=jnp.float32
        )
        x = sw_raw[span].astype(jnp.float32)
        inverse = sw_inv[span]
        pull = (inverse * inverse * inverse) * sum_wide(x * g)
        pgrad_ref[span] = widen(inverse, width) * g - x * widen(pull, width)
        return carry

    over_chunks(grad_pass, 0, 0, half)
    whole(3, 0, others(0, landed)).wait_recv()
    passed[...] = jnp.sum(landed[...], axis=0)
    summed[high] = passed[high]
    spread(3, 1, lambda place: passed.at[place], summed.at[high])
    over_chunks(grad_pass, 0, half, chunks)
    whole(3, 1, others(1, summed)).wait_recv()
    g = jnp.sum(summed[...], axis=0)
    projected = jnp.sum(s_own * g, axis=1, keepdims=True)
    sgrad_ref[...] = s_own_inv * g - s_own * (s_own_inv * s_own_inv * s_own_inv) * projected
    pairs = ((block_rows, rows_buf), (sums1, again1), (sums2, again2), (landed, summed))
    for phase, pair in enumerate(pairs):
        for stage, buffer in enumerate(pair):
            whole(phase, stage, others(stage, buffer)).wait_send()


def body(dp, proto, teacher_rows, student_rows, teacher_protos, student_protos):
    n = dp * proto
    inner = inner_size(n)
    outer = n // inner
    own, width = teacher_rows.shape
    count = teacher_protos.shape[0]
    rows = n * own
    cols = min(count, max(LANES, 65536 // rows))
    f32, bf16 = jnp.float32, jnp.bfloat16
    vmem = pl.BlockSpec(memory_space=pltpu.VMEM)
    hbm = pl.BlockSpec(memory_space=pl.ANY)
    loss, sgrad, pgrad = pl.pallas_call(
        functools.partial(kernel, dp, proto, cols),
        out_shape=(
            jax.ShapeDtypeStruct((1, own), f32),
            jax.ShapeDtypeStruct((own, width), f32),
            pltpu.VMEM((count, width), f32),
        ),
        in_specs=[vmem, vmem, hbm, hbm],
        out_specs=(vmem, vmem, vmem),
        scratch_shapes=[
            pltpu.VMEM((count, width), bf16),
            pltpu.VMEM((count, width), bf16),
            pltpu.VMEM((count, width), bf16),
            pltpu.VMEM((count, width), bf16),
            pltpu.VMEM((count, LANES), f32),
            pltpu.VMEM((rows, count), f32),
            pltpu.VMEM((rows, count), f32),
            pltpu.VMEM((rows, count), f32),
            pltpu.VMEM((rows, count), bf16),
            pltpu.VMEM((outer, inner, 2 * own, width), f32),
            pltpu.VMEM((inner, 1, rows), f32),
            pltpu.VMEM((outer, 1, rows), f32),
            pltpu.VMEM((inner, 3, rows), f32),
            pltpu.VMEM((outer, 3, rows), f32),
            pltpu.VMEM((inner, outer, own, width), f32),
            pltpu.VMEM((inner, outer, own, width), f32),
            pltpu.VMEM((outer, own, width), f32),
            pltpu.VMEM((outer, own, width), f32),
            pltpu.VMEM((rows, width), bf16),
            pltpu.VMEM((rows, width), bf16),
            pltpu.SemaphoreType.DMA((2, LOAD_PARTS)),
            pltpu.SemaphoreType.DMA((4, 2)),
            pltpu.SemaphoreType.DMA((4, 2)),
        ],
        compiler_params=pltpu.CompilerParams(
            collective_id=0, has_side_effects=True, vmem_limit_bytes=56 * 1024 * 1024
        ),
    )(teacher_rows, student_rows, teacher_protos, student_protos)
    return loss.reshape(own), sgrad, pgrad


def solution(mesh):
    spec = P(AXES, None)
    return jax.shard_map(
        functools.partial(body, mesh.shape["dp"], mesh.shape["proto"]),
        mesh=mesh,
        in_specs=(spec,) * 4,
        out_specs=(P(AXES), spec, spec),
        check_vma=False,
    )
```

```python
import functools

import jax
import jax.numpy as jnp
from jax import lax
from jax.experimental import pallas as pl
from jax.experimental.pallas import tpu as pltpu
from jax.sharding import PartitionSpec as P

TEACH_TEMP = 0.04
STUD_TEMP = 0.1
LOSS_SCALE = 4096.0
EPSILON = 1e-06
AXES = ("dp", "proto")
LANES = 128
LOAD_PARTS = 4


def inverse_norm(x):
    return lax.rsqrt(jnp.sum(x * x, axis=-1, keepdims=True) + EPSILON)


def sum_wide(x):
    ones = jnp.ones((x.shape[1], LANES), jnp.bfloat16)
    high = x.astype(jnp.bfloat16)
    low = (x - high.astype(jnp.float32)).astype(jnp.bfloat16)
    return jnp.dot(high, ones, preferred_element_type=jnp.float32) + jnp.dot(
        low, ones, preferred_element_type=jnp.float32
    )


def widen(x, width):
    return jnp.concatenate([x] * (width // LANES), axis=1)


def fold_lanes(x):
    total = x[:, :LANES]
    for start in range(LANES, x.shape[1], LANES):
        total = total + x[:, start:start + LANES]
    return total


def eye():
    shape = (LANES, LANES)
    return lax.broadcasted_iota(jnp.int32, shape, 0) == lax.broadcasted_iota(jnp.int32, shape, 1)


def to_lanes(column):
    blocks = [
        jnp.sum(jnp.where(eye(), column[i:i + LANES], 0.0), axis=0, keepdims=True)
        for i in range(0, column.shape[0], LANES)
    ]
    return blocks[0] if len(blocks) == 1 else jnp.concatenate(blocks, axis=1)


def to_column(row):
    blocks = [
        jnp.sum(jnp.where(eye(), row[:, i:i + LANES], 0.0), axis=1, keepdims=True)
        for i in range(0, row.shape[1], LANES)
    ]
    return blocks[0] if len(blocks) == 1 else jnp.concatenate(blocks, axis=0)


def kernel(
    dp, proto, cols,
    t_ref, s_ref, tw_hbm, sw_hbm,
    loss_ref, sgrad_ref, pgrad_ref,
    tw_raw, sw_raw, tw_unit, sw_unit, sw_inv, texp, logit, sexp, delta,
    rows_buf, sums1, sums2, part, landed, t_all, s_all,
    load_sem, send_sem, recv_sem,
):
    n = dp * proto
    own = t_ref.shape[0]
    total_rows = n * own
    width = t_ref.shape[1]
    count = tw_raw.shape[0]
    chunks = count // cols
    me = lax.axis_index("dp") * proto + lax.axis_index("proto")

    def coords(j):
        peer = lax.rem(me + j, n)
        return peer, (lax.div(peer, proto), lax.rem(peer, proto))

    piece = count // LOAD_PARTS
    loads = []
    for index, (hbm, raw) in enumerate(((tw_hbm, tw_raw), (sw_hbm, sw_raw))):
        for k in range(LOAD_PARTS):
            span = pl.ds(k * piece, piece)
            copy = pltpu.make_async_copy(hbm.at[span], raw.at[span], load_sem.at[index, k])
            copy.start()
            loads.append(copy)

    barrier = pltpu.get_barrier_semaphore()

    @pl.loop(1, n)
    def _(j):
        pl.semaphore_signal(barrier, inc=1, device_id=coords(j)[1], device_id_type=pl.DeviceIdType.MESH)

    t_own = t_ref[...].astype(jnp.float32)
    s_own = s_ref[...].astype(jnp.float32)
    s_own_inv = inverse_norm(s_own)
    t_rounded = (t_own * inverse_norm(t_own)).astype(jnp.bfloat16).astype(jnp.float32)
    s_rounded = (s_own * s_own_inv).astype(jnp.bfloat16).astype(jnp.float32)
    rows_buf[me] = jnp.concatenate([t_rounded, s_rounded], axis=0)
    def spread(phase, source, target):
        @pl.loop(1, n)
        def _(j):
            peer, device = coords(j)
            pltpu.make_async_remote_copy(
                src_ref=source(peer), dst_ref=target.at[me],
                send_sem=send_sem.at[phase], recv_sem=recv_sem.at[phase],
                device_id=device, device_id_type=pl.DeviceIdType.MESH,
            ).start()

    def whole(phase, target):
        span = pl.ds(0, n - 1)
        return pltpu.make_async_remote_copy(
            src_ref=target.at[span], dst_ref=target.at[span],
            send_sem=send_sem.at[phase], recv_sem=recv_sem.at[phase],
            device_id=coords(1)[1], device_id_type=pl.DeviceIdType.MESH,
        )

    norm_rows = min(piece, 512)
    for index, raw in enumerate((tw_raw, sw_raw)):
        if index == 1:
            pl.semaphore_wait(barrier, n - 1)
            spread(0, lambda peer: rows_buf.at[me], rows_buf)
        for k in range(LOAD_PARTS):
            loads[index * LOAD_PARTS + k].wait()

            @pl.loop(0, piece // norm_rows)
            def _(c, k=k, index=index, raw=raw):
                span = pl.ds(pl.multiple_of(k * piece + c * norm_rows, norm_rows), norm_rows)
                x = raw[span].astype(jnp.float32)
                inverse = lax.rsqrt(sum_wide(x * x) + EPSILON)
                unit = (x * widen(inverse, width)).astype(jnp.bfloat16)
                if index == 0:
                    tw_unit[span] = unit
                else:
                    sw_unit[span] = unit
                    sw_inv[span] = inverse

    whole(0, rows_buf).wait_recv()
    paired = rows_buf[...].reshape(n // 2, 2, 2 * own, width)
    first, second = paired[:, 0], paired[:, 1]
    upper = lax.broadcasted_iota(jnp.int32, first.shape, 1) < own
    t_all[...] = jnp.where(upper, first, pltpu.roll(second, own, 1)).reshape(total_rows, width).astype(jnp.bfloat16)
    s_all[...] = jnp.where(upper, pltpu.roll(first, own, 1), second).reshape(total_rows, width).astype(jnp.bfloat16)

    transposed = (((1,), (1,)), ((), ()))
    zeros = jnp.zeros((total_rows, LANES), jnp.float32)

    def span_of(c):
        return pl.ds(c * cols, cols)

    def over_chunks(step, carry):
        for c in range(chunks):
            carry = step(c, carry)
        return carry

    def first_pass(c, carry):
        span = span_of(c)
        expo = jnp.exp(
            lax.dot_general(t_all[...], tw_unit[span], transposed, preferred_element_type=jnp.float32)
            * (1.0 / TEACH_TEMP)
        )
        texp[:, span] = expo
        scale = 1.0 / jnp.sum(expo, axis=0, keepdims=True)
        return carry + fold_lanes(expo * scale)

    def student_pass(c, carry):
        span = span_of(c)
        logits = lax.dot_general(
            s_all[...], sw_unit[span], transposed, preferred_element_type=jnp.float32
        ) * (1.0 / STUD_TEMP)
        logit[:, span] = logits
        expo = jnp.exp(logits)
        sexp[:, span] = expo
        return carry + fold_lanes(expo)

    def send_sums(phase, sums, parts):
        rows = [to_lanes(jnp.sum(x, axis=1, keepdims=True)) for x in parts]
        sums[me] = rows[0] if len(rows) == 1 else jnp.concatenate(rows, axis=0)
        spread(phase, lambda peer: sums.at[me], sums)

    def receive_sums(phase, sums):
        whole(phase, sums).wait_recv()
        return jnp.sum(sums[...], axis=0)

    send_sums(1, sums1, (over_chunks(first_pass, zeros),))
    exp_sum = over_chunks(student_pass, zeros)
    row_total = receive_sums(1, sums1)
    row_scale = to_column(1.0 / row_total)

    def second_pass(c, carry):
        row_sum, dot_sum = carry
        span = span_of(c)
        expo = texp[:, span]
        scale = 1.0 / jnp.sum(expo * row_scale, axis=0, keepdims=True)
        scaled = expo * scale
        texp[:, span] = scaled
        return row_sum + fold_lanes(scaled), dot_sum + fold_lanes(scaled * logit[:, span])

    row_sum, dot_sum = over_chunks(second_pass, (zeros, zeros))
    send_sums(2, sums2, (row_sum, dot_sum, exp_sum))
    total = receive_sums(2, sums2)
    row_total, dot_total, exp_total = total[0:1], total[1:2], total[2:3]
    factor = LOSS_SCALE / STUD_TEMP
    row_scale = to_column(factor / row_total)
    exp_scale = to_column(factor / exp_total)

    def third_pass(c, carry):
        span = span_of(c)
        gradient = (sexp[:, span] * exp_scale - texp[:, span] * row_scale).astype(jnp.bfloat16)
        delta[:, span] = gradient
        return carry + jnp.dot(gradient, sw_unit[span], preferred_element_type=jnp.float32)

    row_part = over_chunks(third_pass, jnp.zeros((total_rows, width), jnp.float32))
    part[...] = row_part.reshape(n, own, width)
    landed[me] = part[me]
    spread(3, lambda peer: part.at[peer], landed)

    loss = jnp.log(exp_total) - dot_total / row_total
    shape = (total_rows, LANES)
    mine = lax.broadcasted_iota(jnp.int32, shape, 0) == me * own + lax.broadcasted_iota(jnp.int32, shape, 1)
    loss_ref[...] = jnp.sum(jnp.where(mine, to_column(loss), 0.0), axis=0, keepdims=True)[:, :own]

    for c in range(chunks):
        span = span_of(c)
        g = lax.dot_general(
            delta[:, span], s_all[...], (((0,), (0,)), ((), ())), preferred_element_type=jnp.float32
        )
        x = sw_raw[span].astype(jnp.float32)
        inverse = sw_inv[span]
        pull = (inverse * inverse * inverse) * sum_wide(x * g)
        pgrad_ref[span] = widen(inverse, width) * g - x * widen(pull, width)

    whole(3, landed).wait_recv()
    g = jnp.sum(landed[...], axis=0)
    projected = jnp.sum(s_own * g, axis=1, keepdims=True)
    sgrad_ref[...] = s_own_inv * g - s_own * (s_own_inv * s_own_inv * s_own_inv) * projected
    for phase, target in enumerate((rows_buf, sums1, sums2, landed)):
        whole(phase, target).wait_send()


def body(dp, proto, teacher_rows, student_rows, teacher_protos, student_protos):
    n = dp * proto
    own, width = teacher_rows.shape
    count = teacher_protos.shape[0]
    rows = n * own
    cols = min(count, max(LANES, 65536 // rows))
    f32, bf16 = jnp.float32, jnp.bfloat16
    vmem = pl.BlockSpec(memory_space=pltpu.VMEM)
    hbm = pl.BlockSpec(memory_space=pl.ANY)
    loss, sgrad, pgrad = pl.pallas_call(
        functools.partial(kernel, dp, proto, cols),
        out_shape=(
            jax.ShapeDtypeStruct((1, own), f32),
            jax.ShapeDtypeStruct((own, width), f32),
            pltpu.VMEM((count, width), f32),
        ),
        in_specs=[vmem, vmem, hbm, hbm],
        out_specs=(vmem, vmem, vmem),
        scratch_shapes=[
            pltpu.VMEM((count, width), bf16),
            pltpu.VMEM((count, width), bf16),
            pltpu.VMEM((count, width), bf16),
            pltpu.VMEM((count, width), bf16),
            pltpu.VMEM((count, LANES), f32),
            pltpu.VMEM((rows, count), f32),
            pltpu.VMEM((rows, count), f32),
            pltpu.VMEM((rows, count), f32),
            pltpu.VMEM((rows, count), bf16),
            pltpu.VMEM((n, 2 * own, width), f32),
            pltpu.VMEM((n, 1, rows), f32),
            pltpu.VMEM((n, 3, rows), f32),
            pltpu.VMEM((n, own, width), f32),
            pltpu.VMEM((n, own, width), f32),
            pltpu.VMEM((rows, width), bf16),
            pltpu.VMEM((rows, width), bf16),
            pltpu.SemaphoreType.DMA((2, LOAD_PARTS)),
            pltpu.SemaphoreType.DMA((4,)),
            pltpu.SemaphoreType.DMA((4,)),
        ],
        compiler_params=pltpu.CompilerParams(
            collective_id=0, has_side_effects=True, vmem_limit_bytes=56 * 1024 * 1024
        ),
    )(teacher_rows, student_rows, teacher_protos, student_protos)
    return loss.reshape(own), sgrad, pgrad


def solution(mesh):
    spec = P(AXES, None)
    return jax.shard_map(
        functools.partial(body, mesh.shape["dp"], mesh.shape["proto"]),
        mesh=mesh,
        in_specs=(spec,) * 4,
        out_specs=(P(AXES), spec, spec),
        check_vma=False,
    )
```
